32 devices in a mesh: row: 2 (over x), col: 16 (over z, y, core).
Axes of the slice: x: 2, y: 2, z: 4, core: 2. Of those that a mesh axis runs over, the one named last changes fastest.
Arguments:
- features: float32 [16, 1024, 128], P('col'), may hold values from -6 to 6
- self_weight: float32 [128, 256], replicated, may hold values from -0.5 to 0.5
- neigh_weight: float32 [128, 256], replicated, may hold values from -0.5 to 0.5
- bias: float32 [256], replicated, may hold values from -4 to 4
- edge_tiles: bfloat16 [2, 16, 96, 128, 128], P('row', 'col'), may hold values from -0.15625 to 0.15625
- tile_rows: int32 [2, 16, 96], P('row', 'col'), may hold values from 0 to 7
- tile_cols: int32 [2, 16, 96], P('row', 'col'), may hold values from 0 to 7
- tile_count: int32 [2, 16, 8], P('row', 'col'), may hold values from 1 to 12, as said below
- cotangent: float32 [16, 1024, 256], P('col', 'row'), may hold values from -6 to 6
Outputs:
- output: float32 [16, 1024, 256], P('col', 'row')
- grad_self: float32 [128, 256], replicated
- grad_neigh: float32 [128, 256], replicated
- grad_bias: float32 [256], replicated
The draws below stay inside these ranges and needn't reach their ends.
Inputs may be any that keep to these rules, and one draw needn't show every extreme that they name: tile_count reaches 12 in every draw.
All inputs are finite; a program needn't handle non-finite values.
Results may differ from the reference program's by a relative error of at most 0.0003.
Values sent between devices are 32-bit elements; how exact they have to be, the bound alone decides.
No kernel may reach another device: no remote copies, remote signals or barrier semaphores. Data moves between devices by JAX's collectives and lax.ppermute only.
A program may use at most 64 MiB of HBM per device.

```python
import jax
import jax.numpy as jnp
from jax import lax

DIN = 128
DOUT = 256
TILE = 128
KT = 8
TS = 12
STOPS = 8
G = 1024
NODES = 16384
N_ROW = 2
N_COL = 16


def draw_tile_count(key, part):
    counts = jax.random.randint(key, (N_ROW, N_COL, STOPS), 1, TS + 1)
    return counts.at[0, 0, 0].set(TS).astype(jnp.int32)


def plant(drawn, own_key, low, high):
    longest = drawn.shape.index(max(drawn.shape))
    spots = []
    for shift in (0, 1):
        where = [jax.random.randint(jax.random.fold_in(own_key, axis), (), 0, length) for axis, length in enumerate(drawn.shape)]
        where[longest] = (where[longest] + shift) % drawn.shape[longest]
        spots.append(tuple(where))
    return drawn.at[spots[0]].set(low).at[spots[1]].set(high)


def steps_of(key, dims, pieces, low, top_value):
    factor_of = 1.0
    for axis_at, blocks in pieces:
        draws = jax.random.uniform(jax.random.fold_in(jax.random.fold_in(key, 6), axis_at), (blocks,), jnp.float32, low / len(pieces), top_value / len(pieces))
        factor_of = factor_of * jnp.repeat(jnp.exp(draws), dims[axis_at] // blocks).reshape((-1,) + (1,) * (len(dims) - 1 - axis_at))
    return factor_of


def centred(rng, dims, spread, most, pieces=(), kind=jnp.bfloat16):
    drawn = jax.random.normal(rng, dims, jnp.float32) * spread
    if len(pieces) > 0:
        drawn = steps_of(rng, dims, pieces, -0.22, 0.18) * drawn
    return jnp.clip(drawn, min=-most, max=most).astype(kind)


def setup_inputs(seed: int = 0) -> dict:
    seeds = jax.random.split(jax.random.key(seed), 10)
    return {
        "features": centred(seeds[0], (N_COL, G, DIN), 1.0, 6.0, ((0, 16),), jnp.float32),
        "self_weight": centred(seeds[1], (DIN, DOUT), DIN ** -0.5, 0.5, (), jnp.float32),
        "neigh_weight": centred(seeds[2], (DIN, DOUT), DIN ** -0.5, 0.5, (), jnp.float32),
        "bias": centred(seeds[3], (DOUT,), 0.7, 4.0, (), jnp.float32),
        "edge_tiles": centred(seeds[4], (N_ROW, N_COL, STOPS * TS, TILE, TILE), (N_ROW * STOPS * TS * TILE // (2 * KT)) ** -0.5, 0.15625, ((0, 2), (1, 16))),
        "tile_rows": plant(jax.random.randint(seeds[5], (N_ROW, N_COL, STOPS * TS), 0, KT), jax.random.fold_in(seeds[5], 1), 0, KT - 1).astype(jnp.int32),
        "tile_cols": plant(jax.random.randint(seeds[6], (N_ROW, N_COL, STOPS * TS), 0, KT), jax.random.fold_in(seeds[6], 1), 0, KT - 1).astype(jnp.int32),
        "tile_count": draw_tile_count(jax.random.fold_in(seeds[9], 71), 0),
        "cotangent": centred(seeds[8], (N_COL, G, DOUT), 1.0, 6.0, ((0, 16), (1, 2)), jnp.float32),
    }


def layer(params, own, agg):
    self_weight, neigh_weight, bias = params
    pre = jnp.dot(own, self_weight, precision=lax.Precision.HIGHEST) + jnp.dot(agg, neigh_weight, precision=lax.Precision.HIGHEST) + bias
    hidden = jax.nn.gelu(pre, approximate=True)
    scale = lax.rsqrt(lax.optimization_barrier(jnp.mean(hidden * hidden, axis=-1, keepdims=True)) + 1e-06)
    return hidden * scale

def device_partial(r, c, features, edge_tiles, tile_rows, tile_cols, tile_count):
    tiles = edge_tiles[r, c].reshape(STOPS, TS, TILE, TILE)
    rows_idx = tile_rows[r, c].reshape(STOPS, TS)
    cols_idx = tile_cols[r, c].reshape(STOPS, TS)
    counts = tile_count[r, c]

    def one_stop(total, s):
        j = jnp.mod(c - r * STOPS - s, N_COL).astype(jnp.int32)
        block = features[j].reshape(KT, TILE, DIN)
        chosen = block[cols_idx[s]]
        live = (jnp.arange(TS, dtype=jnp.int32) < counts[s]).astype(jnp.float32)
        weights = tiles[s].astype(jnp.float32) * live[:, None, None]
        prod = jnp.einsum('tij,tjd->tid', weights, chosen, precision=lax.Precision.HIGHEST)
        return (total.at[rows_idx[s]].add(prod), None)
    start = jnp.zeros((KT, TILE, DIN), jnp.float32)
    total, _ = lax.scan(one_stop, start, jnp.arange(STOPS, dtype=jnp.int32))
    return total.reshape(G, DIN)

def reference(features, self_weight, neigh_weight, bias, edge_tiles, tile_rows, tile_cols, tile_count, cotangent):

    def block_sum(c):
        parts = jax.vmap(lambda r: device_partial(r, c, features, edge_tiles, tile_rows, tile_cols, tile_count))(jnp.arange(N_ROW, dtype=jnp.int32))
        return lax.optimization_barrier(jnp.sum(parts, axis=0))
    aggregate = lax.map(block_sum, jnp.arange(N_COL, dtype=jnp.int32))
    own = features.reshape(NODES, DIN)
    agg = aggregate.reshape(NODES, DIN)
    output, pullback = jax.vjp(lambda p: layer(p, own, agg), (self_weight, neigh_weight, bias))
    grads = pullback(cotangent.reshape(NODES, DOUT))[0]
    return (output.reshape(N_COL, G, DOUT), grads[0], grads[1], grads[2])
```

```python
import functools

import jax
import jax.numpy as jnp
from jax import lax
from jax.experimental import pallas as pl
from jax.experimental.pallas import tpu as pltpu
from jax.sharding import PartitionSpec as P

VMEM = pltpu.VMEM
SMEM = pltpu.SMEM
F32 = jnp.float32
BF16 = jnp.bfloat16
LIMIT = 48 * 1024 * 1024
GROUP = 4


def split(value):
    high = value.astype(BF16)
    low = (value - high.astype(F32)).astype(BF16)
    return high, low


def dot3(left, right, dims):
    lh, ll = left
    rh, rl = right
    mul = functools.partial(
        lax.dot_general, dimension_numbers=(dims, ((), ())), preferred_element_type=F32
    )
    return mul(lh, rh) + (mul(lh, rl) + mul(ll, rh))


def spec(space):
    return pl.BlockSpec(memory_space=space)


def tiles_kernel(
    parts, halved, has_acc, n_half, slots, side,
    meta, rows, cols, counts, *refs,
):
    n_in = sum(2 if h else 1 for h in halved)
    blocks, refs = refs[:n_in], refs[n_in:]
    tiles, refs = refs[0], refs[1:]
    if has_acc:
        acc_in, refs = refs[0], refs[1:]
    if n_half:
        keep, send, acc, pair, buf, sems = refs
    else:
        acc, pair, buf, sems = refs

    def copy(b):
        stop = jnp.maximum(meta[b], 0)
        return pltpu.make_async_copy(
            tiles.at[pl.ds(stop * slots, slots)], buf.at[b], sems.at[b]
        )

    for b in range(parts):
        copy(b).start()
    if has_acc:
        acc[...] = acc_in[...]
    else:
        acc[...] = jnp.zeros_like(acc)
    width = acc.shape[1]
    at = 0
    for b in range(parts):
        stop = meta[b]
        slot = b % 2
        if halved[b]:
            mine, other = blocks[at], blocks[at + 1]
            at += 2
            half = mine.shape[0]
            core = meta[parts]
            for ref, place in ((mine, core), (other, 1 - core)):
                high, low = split(ref[...])
                start = pl.multiple_of(place * half, half)
                pair[slot, pl.ds(start, half), :width] = high
                pair[slot, pl.ds(start, half), width:] = low
        else:
            high, low = split(blocks[at][...])
            at += 1
            pair[slot, :, :width] = high
            pair[slot, :, width:] = low
        copy(b).wait()
        safe = jnp.maximum(stop, 0)
        count = jnp.where(stop >= 0, counts[safe], 0)
        base = safe * slots
        for first in range(0, slots, GROUP):
            here = range(first, min(first + GROUP, slots))

            @pl.when(first < count)
            def _(b=b, slot=slot, here=here, base=base, count=count):
                prods = []
                for t in here:
                    col = pl.multiple_of(cols[base + t] * side, side)
                    both = jnp.dot(
                        buf[b, t], pair[slot, pl.ds(col, side), :],
                        preferred_element_type=F32,
                    )
                    prods.append(both[:, :width] + both[:, width:])
                for t, prod in zip(here, prods):
                    row = pl.multiple_of(rows[base + t] * side, side)
                    acc[pl.ds(row, side), :] += jnp.where(t < count, prod, 0.0)

    if n_half:
        half = keep.shape[0]
        row = meta[parts + 1]
        for out, place in zip((keep, *(send,)), (row, 1 - row)):
            out[...] = acc[pl.ds(pl.multiple_of(place * half, half), half), :]


def add_products(blocks, stops, core, row, index, tiles, acc, finish):
    rows, cols, counts = index
    halved = tuple(isinstance(b, tuple) for b in blocks)
    flat = [a for b in blocks for a in (b if isinstance(b, tuple) else (b,))]
    n = len(blocks)
    nodes = 2 * flat[0].shape[0] if halved[0] else flat[0].shape[0]
    width = flat[0].shape[1]
    slots = tiles.shape[0] // counts.shape[0]
    side = tiles.shape[1]
    meta = jnp.stack([*stops, core, row]).astype(jnp.int32)
    whole = jax.ShapeDtypeStruct((nodes, width), F32)
    part = jax.ShapeDtypeStruct((nodes // 2, width), F32)
    body = functools.partial(
        tiles_kernel, n, halved, acc is not None, int(finish), slots, side
    )
    scratch = [
        VMEM((2, nodes, 2 * width), BF16),
        VMEM((n, slots, side, side), BF16),
        pltpu.SemaphoreType.DMA((n,)),
    ]
    if finish:
        scratch = [VMEM((nodes, width), F32)] + scratch
    return pl.pallas_call(
        body,
        out_shape=(part, part) if finish else whole,
        in_specs=[spec(SMEM)] * 4
        + [spec(VMEM)] * len(flat)
        + [spec(pl.ANY)]
        + ([spec(VMEM)] if acc is not None else []),
        out_specs=(spec(VMEM),) * 2 if finish else spec(VMEM),
        scratch_shapes=scratch,
        compiler_params=pltpu.CompilerParams(vmem_limit_bytes=LIMIT),
        cost_estimate=pl.CostEstimate(
            flops=n * slots * side * side * width * 40,
            bytes_accessed=n * slots * side * side * 2,
            transcendentals=0,
        ),
    )(meta, rows, cols, counts, *flat, tiles, *(() if acc is None else (acc,)))


def layer_kernel(
    core, own, kept, got, self_weight, neigh_weight, bias, cotangent,
    output, keep, send,
):
    depth = self_weight.shape[0]
    units = self_weight.shape[1]
    both = jnp.concatenate([own[...], kept[...] + got[...]], axis=1)
    inputs = split(both)
    weights = split(jnp.concatenate([self_weight[...], neigh_weight[...]], axis=0))
    pre = dot3(inputs, weights, ((1,), (0,))) + bias[...]
    root = 0.7978845608028654
    square = pre * pre
    bend = jnp.tanh(root * (pre + 0.044715 * (square * pre)))
    rise = 0.5 * (1.0 + bend)
    hidden = pre * rise
    scale = lax.rsqrt(jnp.mean(hidden * hidden, axis=-1, keepdims=True) + 1e-06)
    out = hidden * scale
    output[...] = out
    weight = cotangent[...]
    along = jnp.mean(weight * out, axis=-1, keepdims=True)
    slope = rise + (0.5 * root) * pre * (1.0 - bend * bend) * (
        1.0 + (3 * 0.044715) * square
    )
    back = scale * (weight - out * along) * slope
    grads = dot3(inputs, split(back), ((0,), (0,)))
    grad_bias = jnp.sum(back, axis=0, keepdims=True)
    first = core[0] == 0
    tail = jnp.broadcast_to(grad_bias, (8, units))
    keep[:depth, :] = jnp.where(first, grads[:depth], grads[depth:])
    send[:depth, :] = jnp.where(first, grads[depth:], grads[:depth])
    keep[depth:, :] = tail
    send[depth:, :] = tail


def run_layer(core, own, kept, got, self_weight, neigh_weight, bias, cotangent):
    nodes, depth = own.shape
    units = self_weight.shape[1]
    part = jax.ShapeDtypeStruct((depth + 8, units), F32)
    return pl.pallas_call(
        layer_kernel,
        out_shape=(jax.ShapeDtypeStruct((nodes, units), F32), part, part),
        in_specs=[spec(SMEM)] + [spec(VMEM)] * 7,
        out_specs=(spec(VMEM),) * 3,
        compiler_params=pltpu.CompilerParams(vmem_limit_bytes=LIMIT),
        cost_estimate=pl.CostEstimate(
            flops=12 * nodes * 2 * depth * units,
            bytes_accessed=nodes * units * 12,
            transcendentals=nodes * units,
        ),
    )(jnp.reshape(core, (1,)), own, kept, got, self_weight, neigh_weight,
      bias.reshape(1, units), cotangent)


def gather_small(block, row, col, send):
    core = col % 2
    y = (col // 2) % 2
    z = col // 4
    half = block.shape[0] // 2
    swap = lambda value: send(value, lambda r, c: (r, c ^ 1))
    beside = swap(block)
    yield [block, beside], [col, col ^ 1]

    near = send(block, lambda r, c: (r, (c + (4 if r == 0 else 12)) % 16))
    near_col = (col + jnp.where(row == 0, 12, 4)) % 16

    mine = jnp.where(core == 1 - row, block, beside)
    mine = lax.dynamic_slice_in_dim(mine, core * half, half, 0)
    far = send(mine, lambda r, c: (r, c ^ 8))

    level = send(
        block, lambda r, c: (r, c ^ 2) if (c // 2) % 2 == r else None
    )
    level_beside = swap(level)
    yield [level, level_beside], [col ^ 2, col ^ 3]

    near_beside = swap(near)
    yield [near, near_beside], [near_col, near_col ^ 1]
    cross = send(near, lambda r, c: (r, c ^ 2))
    cross_beside = swap(cross)
    yield [cross, cross_beside], [near_col ^ 2, near_col ^ 3]

    place = lambda r, c: (r, (c // 2) % 2)
    over_y = send(far, lambda r, c: (r, c ^ 2) if place(r, c) in ((0, 1), (1, 0)) else None)
    over_x = send(far, lambda r, c: (1, c) if r == 0 else None)
    over_d = send(far, lambda r, c: (1 - r, c ^ 2) if place(r, c) in ((0, 0), (1, 1)) else None)
    base = 4 * ((z + 2) % 4)
    here = 2 * row + y
    far_cols = [
        base + 2 * y + 1 - row,
        jnp.where(here == 0, base + 3, jnp.where(here == 3, base, -1)),
        jnp.where(here == 2, base + 1, jnp.where(here == 3, base + 3, -1)),
        jnp.where(here == 0, base + 2, jnp.where(here == 3, base + 1, -1)),
    ]
    halves = [far, over_y, over_x, over_d]
    yield [(h, swap(h)) for h in halves], far_cols


def gather_ring(block, row, col, send, rows, cols, stops):
    held = send(block, lambda r, c: (r, (c + stops * r) % cols))
    held = jnp.where(row == 0, block, held)
    at = (col - stops * row) % cols
    for stop in range(stops):
        if stop:
            held = send(held, lambda r, c: (r, (c + 1) % cols))
            at = (at - 1) % cols
        yield [held], [at]


def on_device(
    features, self_weight, neigh_weight, bias, edge_tiles, tile_rows, tile_cols,
    tile_count, cotangent,
):
    rows = lax.axis_size("row")
    cols = lax.axis_size("col")
    row = lax.axis_index("row")
    col = lax.axis_index("col")
    stops = tile_count.shape[2]
    block = features[0]
    tiles = edge_tiles[0, 0]
    index = (tile_rows[0, 0], tile_cols[0, 0], tile_count[0, 0])
    small = rows == 2 and cols == 16 and stops == 8

    def send(value, to):
        pairs = []
        for r in range(rows):
            for c in range(cols):
                goal = to(r, c)
                if goal is not None and goal != (r, c):
                    pairs.append((r * cols + c, goal[0] * cols + goal[1]))
        return lax.ppermute(value, ("row", "col"), pairs)

    if small:
        groups = list(gather_small(block, row, col, send))
    else:
        groups = list(gather_ring(block, row, col, send, rows, cols, stops))
    core = col % 2
    acc = None
    for g, (blocks, at) in enumerate(groups):
        which = []
        for column in at:
            stop = (col - stops * row - column) % cols
            which.append(jnp.where((column >= 0) & (stop < stops), stop, -1))
        last = small and g == len(groups) - 1
        acc = add_products(blocks, which, core, row, index, tiles, acc, last)

    share = cotangent.shape[1]
    own = lax.dynamic_slice_in_dim(block, row * share, share, 0)
    if small:
        kept, away = acc
        got = send(away, lambda r, c: (1 - r, c))
    else:
        kept = lax.psum_scatter(acc, "row", scatter_dimension=0, tiled=True)
        got = jnp.zeros_like(kept)
    output, keep, away = run_layer(
        core, own, kept, got, self_weight, neigh_weight, bias, cotangent[0]
    )
    swap = lambda value: send(value, lambda r, c: (r, c ^ 1))
    total = keep + swap(away)
    if small:
        total = total + send(total, lambda r, c: (1 - r, c))
        for bit in (2, 4, 8):
            total = total + send(total, lambda r, c: (r, c ^ bit))
    else:
        total = lax.psum(total, "row")
        bit = 2
        while bit < cols:
            total = total + send(total, lambda r, c: (r, c ^ bit))
            bit *= 2
    other = swap(total)
    depth = self_weight.shape[0]
    first = core == 0
    grad_self = jnp.where(first, total[:depth], other[:depth])
    grad_neigh = jnp.where(first, other[:depth], total[:depth])
    return (output[None], grad_self, grad_neigh, total[depth])


def solution(mesh):
    in_specs = (
        P("col", None, None),
        P(),
        P(),
        P(),
        P("row", "col", None, None, None),
        P("row", "col", None),
        P("row", "col", None),
        P("row", "col", None),
        P("col", "row", None),
    )
    out_specs = (P("col", "row", None), P(), P(), P())
    return jax.shard_map(
        on_device, mesh=mesh, in_specs=in_specs, out_specs=out_specs, check_vma=False
    )
```

```python
import functools

import jax
import jax.numpy as jnp
from jax import lax
from jax.experimental import pallas as pl
from jax.experimental.pallas import tpu as pltpu
from jax.sharding import PartitionSpec as P

VMEM = pltpu.VMEM
SMEM = pltpu.SMEM
F32 = jnp.float32
BF16 = jnp.bfloat16
LIMIT = 24 * 1024 * 1024
GROUP = 4
COST = 10


def split(value):
    high = value.astype(BF16)
    low = (value - high.astype(F32)).astype(BF16)
    return high, low


def dot3(left, right, dims):
    lh, ll = left
    rh, rl = right
    mul = functools.partial(
        lax.dot_general, dimension_numbers=(dims, ((), ())), preferred_element_type=F32
    )
    return mul(lh, rh) + (mul(lh, rl) + mul(ll, rh))


def spec(space):
    return pl.BlockSpec(memory_space=space)


def tiles_kernel(goals, pieces, has_acc, finish, slots, stops, rows, cols, counts, *refs):
    blocks = []
    for count in pieces:
        blocks.append(refs[:count])
        refs = refs[count:]
    tiles, refs = refs[0], refs[1:]
    if has_acc:
        acc_in, refs = refs[0], refs[1:]
    if finish:
        keep, send, acc, pair = refs
    else:
        acc, pair = refs
    row = lax.axis_index("row")
    col = lax.axis_index("col")
    across = lax.axis_size("col")
    if has_acc:
        acc[...] = acc_in[...]
    else:
        acc[...] = jnp.zeros_like(acc)
    width = acc.shape[1]
    side = tiles.shape[1]
    for goal, block in zip(goals, blocks):
        stop = lax.rem(col - stops * row - goal(row, col) + 2 * across, across)

        @pl.when(stop < stops)
        def _(block=block, stop=stop):
            for place, piece in enumerate(block):
                high, low = split(piece[...].reshape(-1, width))
                size = high.shape[0]
                if len(block) == 1:
                    start = 0
                else:
                    start = pl.multiple_of((1 - row if place else row) * size, size)
                pair[pl.ds(start, size), :width] = high
                pair[pl.ds(start, size), width:] = low
            live = counts[0, 0, stop]
            base = stop * slots
            for first in range(0, slots, GROUP):
                here = range(first, min(first + GROUP, slots))

                @pl.when(first < live)
                def _(here=here):
                    prods = []
                    for t in here:
                        at = pl.multiple_of(cols[0, 0, base + t] * side, side)
                        both = jnp.dot(
                            tiles[base + t], pair[pl.ds(at, side), :],
                            preferred_element_type=F32,
                        )
                        prods.append(both[:, :width] + both[:, width:])
                    for t, prod in zip(here, prods):
                        at = pl.multiple_of(rows[0, 0, base + t] * side, side)
                        acc[pl.ds(at, side), :] += jnp.where(t < live, prod, 0.0)

    if finish:
        half = keep.shape[0]
        for out, place in ((keep, row), (send, 1 - row)):
            out[...] = acc[pl.ds(pl.multiple_of(place * half, half), half), :]


def add_products(blocks, goals, index, stops, tiles, acc, finish):
    blocks = [b if isinstance(b, tuple) else (b,) for b in blocks]
    pieces = tuple(len(b) for b in blocks)
    flat = [piece for b in blocks for piece in b]
    n = len(blocks)
    width = flat[0].shape[-1]
    nodes = sum(piece.size for piece in blocks[0]) // width
    slots = tiles.shape[0] // stops
    side = tiles.shape[1]
    whole = jax.ShapeDtypeStruct((nodes, width), F32)
    part = jax.ShapeDtypeStruct((nodes // 2, width), F32)
    body = functools.partial(
        tiles_kernel, tuple(goals), pieces, acc is not None, finish, slots, stops
    )
    scratch = [VMEM((nodes, 2 * width), BF16)]
    if finish:
        scratch = [VMEM((nodes, width), F32)] + scratch
    return pl.pallas_call(
        body,
        out_shape=(part, part) if finish else whole,
        in_specs=[spec(SMEM)] * 3
        + [spec(VMEM)] * (len(flat) + 1)
        + ([spec(VMEM)] if acc is not None else []),
        out_specs=(spec(VMEM),) * 2 if finish else spec(VMEM),
        scratch_shapes=scratch,
        compiler_params=pltpu.CompilerParams(vmem_limit_bytes=LIMIT),
        cost_estimate=pl.CostEstimate(
            flops=n * slots * side * side * width * COST,
            bytes_accessed=n * slots * side * side * 2,
            transcendentals=0,
        ),
    )(*index, *flat, tiles, *(() if acc is None else (acc,)))


def half_kernel(block, out):
    half = out.shape[0]
    at = pl.multiple_of(lax.axis_index("row") * half, half)
    out[...] = block[0, pl.ds(at, half), :]


def row_half(block):
    _, nodes, width = block.shape
    return pl.pallas_call(
        half_kernel,
        out_shape=jax.ShapeDtypeStruct((nodes // 2, width), F32),
        in_specs=[spec(VMEM)],
        out_specs=spec(VMEM),
        compiler_params=pltpu.CompilerParams(vmem_limit_bytes=LIMIT),
    )(block)


def gate_kernel(value, _, out):
    out[...] = value[...]


def gate(value, after):
    return pl.pallas_call(
        gate_kernel,
        out_shape=jax.ShapeDtypeStruct(value.shape, F32),
        in_specs=[spec(VMEM), spec(pl.ANY)],
        out_specs=spec(VMEM),
        compiler_params=pltpu.CompilerParams(vmem_limit_bytes=LIMIT),
        cost_estimate=pl.CostEstimate(
            flops=1024, bytes_accessed=8 * value.size, transcendentals=0
        ),
    )(value, after)


def layer_kernel(
    block, kept, got, self_weight, neigh_weight, bias, cotangent, output, keep, send
):
    depth = self_weight.shape[0]
    units = self_weight.shape[1]
    nodes = kept.shape[0]
    own = block[0, pl.ds(pl.multiple_of(lax.axis_index("row") * nodes, nodes), nodes), :]
    both = jnp.concatenate([own, kept[...] + got[...]], axis=1)
    inputs = split(both)
    weights = split(jnp.concatenate([self_weight[...], neigh_weight[...]], axis=0))
    pre = dot3(inputs, weights, ((1,), (0,))) + bias[...].reshape(1, units)
    root = 0.7978845608028654
    square = pre * pre
    bend = jnp.tanh(root * (pre + 0.044715 * (square * pre)))
    rise = 0.5 * (1.0 + bend)
    hidden = pre * rise
    scale = lax.rsqrt(jnp.mean(hidden * hidden, axis=-1, keepdims=True) + 1e-06)
    out = hidden * scale
    output[0] = out
    weight = cotangent[0]
    along = jnp.mean(weight * out, axis=-1, keepdims=True)
    slope = rise + (0.5 * root) * pre * (1.0 - bend * bend) * (
        1.0 + (3 * 0.044715) * square
    )
    back = scale * (weight - out * along) * slope
    grads = dot3(inputs, split(back), ((0,), (0,)))
    grad_bias = jnp.sum(back, axis=0, keepdims=True)
    first = lax.rem(lax.axis_index("col"), 2) == 0
    tail = jnp.broadcast_to(grad_bias, (8, units))
    keep[:depth, :] = jnp.where(first, grads[:depth], grads[depth:])
    send[:depth, :] = jnp.where(first, grads[depth:], grads[:depth])
    keep[depth:, :] = tail
    send[depth:, :] = tail


def run_layer(block, kept, got, self_weight, neigh_weight, bias, cotangent):
    nodes, depth = kept.shape
    units = self_weight.shape[1]
    part = jax.ShapeDtypeStruct((depth + 8, units), F32)
    return pl.pallas_call(
        layer_kernel,
        out_shape=(jax.ShapeDtypeStruct((1, nodes, units), F32), part, part),
        in_specs=[spec(VMEM)] * 7,
        out_specs=(spec(VMEM),) * 3,
        compiler_params=pltpu.CompilerParams(vmem_limit_bytes=LIMIT),
        cost_estimate=pl.CostEstimate(
            flops=12 * nodes * 2 * depth * units,
            bytes_accessed=nodes * units * 12,
            transcendentals=nodes * units,
        ),
    )(block, kept, got, self_weight, neigh_weight, bias, cotangent)


def grads_kernel(total, other, grad_self, grad_neigh, grad_bias):
    depth = grad_self.shape[0]
    first = lax.rem(lax.axis_index("col"), 2) == 0
    mine, theirs = total[:depth, :], other[:depth, :]
    grad_self[...] = jnp.where(first, mine, theirs)
    grad_neigh[...] = jnp.where(first, theirs, mine)
    grad_bias[...] = total[depth, :]


def place_grads(total, other):
    depth, units = total.shape[0] - 8, total.shape[1]
    part = jax.ShapeDtypeStruct((depth, units), F32)
    return pl.pallas_call(
        grads_kernel,
        out_shape=(part, part, jax.ShapeDtypeStruct((units,), F32)),
        in_specs=[spec(VMEM)] * 2,
        out_specs=(spec(VMEM),) * 3,
        compiler_params=pltpu.CompilerParams(vmem_limit_bytes=LIMIT),
    )(total, other)


def gather_small(block, send, add):
    swap = lambda value: send(value, lambda r, c: (r, c ^ 1))
    near_of = lambda r, c: lax.rem(c + 12 - 8 * r, 16)
    near = send(block, lambda r, c: (r, (c + (4 if r == 0 else 12)) % 16))
    far = send(row_half(block), lambda r, c: (r, c ^ 8))
    level = send(block, lambda r, c: (r, c ^ 2) if (c // 2) % 2 == r else None)
    beside = swap(block)
    cross = send(near, lambda r, c: (r, c ^ 2))
    level_beside = swap(level)
    near_beside = swap(near)
    over_x = send(far, lambda r, c: (1 - r, c))
    over_y = send(far, lambda r, c: (r, c ^ 2))
    over_d = send(far, lambda r, c: (1 - r, c ^ 2))
    acc = add(
        [block, beside, near, near_beside, level, level_beside],
        [
            lambda r, c: c, lambda r, c: c ^ 1, near_of,
            lambda r, c: near_of(r, c) ^ 1, lambda r, c: c ^ 2, lambda r, c: c ^ 3,
        ],
    )
    over_d = gate(over_d, acc)
    acc = add(
        [(far, over_x), (swap(far), swap(over_x)),
         (over_y, over_d), (swap(over_y), swap(over_d))],
        [lambda r, c, bits=bits: c ^ bits for bits in (8, 9, 10, 11)], acc,
    )
    return add(
        [cross, swap(cross)],
        [lambda r, c: near_of(r, c) ^ 2, lambda r, c: near_of(r, c) ^ 3], acc, True,
    )


def gather_ring(block, send, add, rows, cols, stops):
    held = send(block, lambda r, c: (r, (c + stops * r) % cols))
    held = jnp.where(lax.axis_index("row") == 0, block, held)
    acc = None
    for stop in range(stops):
        if stop:
            held = send(held, lambda r, c: (r, (c + 1) % cols))
        at = lambda r, c, stop=stop: lax.rem(c - stops * r - stop + 2 * cols, cols)
        acc = add([held], [at], acc)
    return acc


def on_device(
    features, self_weight, neigh_weight, bias, edge_tiles, tile_rows, tile_cols,
    tile_count, cotangent,
):
    rows = lax.axis_size("row")
    cols = lax.axis_size("col")
    stops = tile_count.shape[2]
    tiles = edge_tiles[0, 0]
    index = (tile_rows, tile_cols, tile_count)
    small = rows == 2 and cols == 16 and stops == 8

    def send(value, to):
        pairs = []
        for r in range(rows):
            for c in range(cols):
                goal = to(r, c)
                if goal is not None and goal != (r, c):
                    pairs.append((r * cols + c, goal[0] * cols + goal[1]))
        return lax.ppermute(value, ("row", "col"), pairs)

    def add(blocks, goals, acc=None, finish=False):
        return add_products(blocks, goals, index, stops, tiles, acc, finish)

    if small:
        kept, away = gather_small(features, send, add)
        got = send(away, lambda r, c: (1 - r, c))
    else:
        acc = gather_ring(features, send, add, rows, cols, stops)
        kept = lax.psum_scatter(acc, "row", scatter_dimension=0, tiled=True)
        got = jnp.zeros_like(kept)
    output, keep, away = run_layer(
        features, kept, got, self_weight, neigh_weight, bias, cotangent
    )
    swap = lambda value: send(value, lambda r, c: (r, c ^ 1))
    total = keep + swap(away)
    if small:
        total = total + send(total, lambda r, c: (1 - r, c))
    else:
        total = lax.psum(total, "row")
    bit = 2
    while bit < cols:
        total = total + send(total, lambda r, c: (r, c ^ bit))
        bit *= 2
    return (output, *place_grads(total, swap(total)))


def solution(mesh):
    in_specs = (
        P("col", None, None),
        P(),
        P(),
        P(),
        P("row", "col", None, None, None),
        P("row", "col", None),
        P("row", "col", None),
        P("row", "col", None),
        P("col", "row", None),
    )
    out_specs = (P("col", "row", None), P(), P(), P())
    return jax.shard_map(
        on_device, mesh=mesh, in_specs=in_specs, out_specs=out_specs, check_vma=False
    )
```

```python
import functools

import jax
import jax.numpy as jnp
from jax import lax
from jax.experimental import pallas as pl
from jax.experimental.pallas import tpu as pltpu
from jax.sharding import PartitionSpec as P

VMEM = pltpu.VMEM
SMEM = pltpu.SMEM
F32 = jnp.float32
BF16 = jnp.bfloat16
LIMIT = 24 * 1024 * 1024
GROUP = 4
COST = 10


def split(value):
    high = value.astype(BF16)
    low = (value - high.astype(F32)).astype(BF16)
    return high, low


def dot3(left, right, dims):
    lh, ll = left
    rh, rl = right
    mul = functools.partial(
        lax.dot_general, dimension_numbers=(dims, ((), ())), preferred_element_type=F32
    )
    return mul(lh, rh) + (mul(lh, rl) + mul(ll, rh))


def spec(space):
    return pl.BlockSpec(memory_space=space)


def tiles_kernel(goals, pieces, has_acc, finish, slots, stops, rows, cols, counts, *refs):
    blocks = []
    for count in pieces:
        if count < 0:
            blocks += [(refs[0].at[at],) for at in range(-count)]
            refs = refs[1:]
        else:
            blocks.append(refs[:count])
            refs = refs[count:]
    tiles, refs = refs[0], refs[1:]
    if has_acc:
        acc_in, refs = refs[0], refs[1:]
    if finish:
        keep, send, acc, pair = refs
    else:
        acc, pair = refs
    row = lax.axis_index("row")
    col = lax.axis_index("col")
    across = lax.axis_size("col")
    if not has_acc:
        acc[...] = jnp.zeros_like(acc)
    elif finish:
        acc[...] = acc_in[...]
    width = acc.shape[1]
    side = tiles.shape[1]
    for goal, block in zip(goals, blocks):
        stop = lax.rem(col - stops * row - goal(row, col) + 2 * across, across)

        @pl.when(stop < stops)
        def _(block=block, stop=stop):
            for place, piece in enumerate(block):
                high, low = split(piece[...])
                size = high.shape[0]
                if len(block) == 1:
                    start = 0
                else:
                    start = pl.multiple_of((1 - row if place else row) * size, size)
                pair[pl.ds(start, size), :width] = high
                pair[pl.ds(start, size), width:] = low
            live = counts[0, 0, stop]
            base = stop * slots
            for first in range(0, slots, GROUP):
                here = range(first, min(first + GROUP, slots))

                @pl.when(first < live)
                def _(here=here):
                    prods = []
                    for t in here:
                        at = pl.multiple_of(cols[0, 0, base + t] * side, side)
                        both = jnp.dot(
                            tiles[base + t], pair[pl.ds(at, side), :],
                            preferred_element_type=F32,
                        )
                        prods.append(both[:, :width] + both[:, width:])
                    for t, prod in zip(here, prods):
                        at = pl.multiple_of(rows[0, 0, base + t] * side, side)
                        acc[pl.ds(at, side), :] += jnp.where(t < live, prod, 0.0)

    if finish:
        half = keep.shape[0]
        for out, place in ((keep, row), (send, 1 - row)):
            out[...] = acc[pl.ds(pl.multiple_of(place * half, half), half), :]


def add_products(blocks, goals, index, stops, tiles, acc, finish, cost):
    blocks = [b if isinstance(b, tuple) else (b,) for b in blocks]
    pieces = tuple(len(b) if len(b) > 1 else -b[0].shape[0] for b in blocks)
    flat = [piece for b in blocks for piece in b]
    n = len(goals)
    width = flat[0].shape[-1]
    nodes = max(len(b) * b[0].shape[-2] for b in blocks)
    slots = tiles.shape[0] // stops
    side = tiles.shape[1]
    whole = jax.ShapeDtypeStruct((nodes, width), F32)
    part = jax.ShapeDtypeStruct((nodes // 2, width), F32)
    body = functools.partial(
        tiles_kernel, tuple(goals), pieces, acc is not None, finish, slots, stops
    )
    scratch = [VMEM((nodes, 2 * width), BF16)]
    if finish:
        scratch = [VMEM((nodes, width), F32)] + scratch
    return pl.pallas_call(
        body,
        out_shape=(part, part) if finish else whole,
        in_specs=[spec(SMEM)] * 3
        + [spec(VMEM)] * (len(flat) + 1)
        + ([spec(VMEM)] if acc is not None else []),
        out_specs=(spec(VMEM),) * 2 if finish else spec(VMEM),
        scratch_shapes=scratch,
        input_output_aliases={} if finish or acc is None else {len(flat) + 4: 0},
        compiler_params=pltpu.CompilerParams(vmem_limit_bytes=LIMIT),
        cost_estimate=pl.CostEstimate(
            flops=n * slots * side * side * width * cost,
            bytes_accessed=n * slots * side * side * 2,
            transcendentals=0,
        ),
    )(*index, *flat, tiles, *(() if acc is None else (acc,)))


def half_kernel(block, out):
    half = out.shape[0]
    row = lax.axis_index("row")
    at = pl.multiple_of(row * half, half)
    out[...] = block[0, pl.ds(at, half), :]


def row_half(block):
    _, nodes, width = block.shape
    return pl.pallas_call(
        half_kernel,
        out_shape=jax.ShapeDtypeStruct((nodes // 2, width), F32),
        in_specs=[spec(VMEM)],
        out_specs=spec(VMEM),
        compiler_params=pltpu.CompilerParams(vmem_limit_bytes=LIMIT),
    )(block)


ROW, OTHER = "row", "other"


def bundle_kernel(places, *refs):
    out = refs[-1]
    row = lax.axis_index("row")
    for ref, (block, half) in zip(refs, places):
        if half is None:
            out[block] = ref[0]
            continue
        size = ref.shape[0]
        half = {ROW: row, OTHER: 1 - row}.get(half, half)
        out[block, pl.ds(pl.multiple_of(half * size, size), size), :] = ref[...]


def bundle(pieces, blocks, after=()):
    piece, (_, half) = pieces[0]
    nodes, width = piece.shape[-2] * (1 if half is None else 2), piece.shape[-1]
    return pl.pallas_call(
        functools.partial(bundle_kernel, tuple(place for _, place in pieces)),
        out_shape=jax.ShapeDtypeStruct((blocks, nodes, width), F32),
        in_specs=[spec(VMEM)] * len(pieces) + [spec(pl.ANY)] * len(after),
        out_specs=spec(VMEM),
        compiler_params=pltpu.CompilerParams(vmem_limit_bytes=LIMIT),
        cost_estimate=pl.CostEstimate(
            flops=1024, bytes_accessed=8 * nodes * width * blocks, transcendentals=0
        ),
    )(*[piece for piece, _ in pieces], *after)


def layer_kernel(
    block, kept, got, self_weight, neigh_weight, bias, cotangent, output, keep, send
):
    depth = self_weight.shape[0]
    units = self_weight.shape[1]
    nodes = kept.shape[0]
    own = block[0, pl.ds(pl.multiple_of(lax.axis_index("row") * nodes, nodes), nodes), :]
    both = jnp.concatenate([own, kept[...] + got[...]], axis=1)
    inputs = split(both)
    weights = split(jnp.concatenate([self_weight[...], neigh_weight[...]], axis=0))
    pre = dot3(inputs, weights, ((1,), (0,))) + bias[...].reshape(1, units)
    root = 0.7978845608028654
    square = pre * pre
    bend = jnp.tanh(root * (pre + 0.044715 * (square * pre)))
    rise = 0.5 * (1.0 + bend)
    hidden = pre * rise
    scale = lax.rsqrt(jnp.mean(hidden * hidden, axis=-1, keepdims=True) + 1e-06)
    out = hidden * scale
    output[0] = out
    weight = cotangent[0]
    along = jnp.mean(weight * out, axis=-1, keepdims=True)
    slope = rise + (0.5 * root) * pre * (1.0 - bend * bend) * (
        1.0 + (3 * 0.044715) * square
    )
    back = scale * (weight - out * along) * slope
    grads = dot3(inputs, split(back), ((0,), (0,)))
    grad_bias = jnp.sum(back, axis=0, keepdims=True)
    first = lax.rem(lax.axis_index("col"), 2) == 0
    tail = jnp.broadcast_to(grad_bias, (8, units))
    keep[:depth, :] = jnp.where(first, grads[:depth], grads[depth:])
    send[:depth, :] = jnp.where(first, grads[depth:], grads[:depth])
    keep[depth:, :] = tail
    send[depth:, :] = tail


def run_layer(block, kept, got, self_weight, neigh_weight, bias, cotangent):
    nodes, depth = kept.shape
    units = self_weight.shape[1]
    part = jax.ShapeDtypeStruct((depth + 8, units), F32)
    return pl.pallas_call(
        layer_kernel,
        out_shape=(jax.ShapeDtypeStruct((1, nodes, units), F32), part, part),
        in_specs=[spec(VMEM)] * 7,
        out_specs=(spec(VMEM),) * 3,
        compiler_params=pltpu.CompilerParams(vmem_limit_bytes=LIMIT),
        cost_estimate=pl.CostEstimate(
            flops=12 * nodes * 2 * depth * units,
            bytes_accessed=nodes * units * 12,
            transcendentals=nodes * units,
        ),
    )(block, kept, got, self_weight, neigh_weight, bias, cotangent)


def grads_kernel(total, other, grad_self, grad_neigh, grad_bias):
    depth = grad_self.shape[0]
    first = lax.rem(lax.axis_index("col"), 2) == 0
    mine, theirs = total[:depth, :], other[:depth, :]
    grad_self[...] = jnp.where(first, mine, theirs)
    grad_neigh[...] = jnp.where(first, theirs, mine)
    grad_bias[...] = total[depth, :]


def place_grads(total, other):
    depth, units = total.shape[0] - 8, total.shape[1]
    part = jax.ShapeDtypeStruct((depth, units), F32)
    return pl.pallas_call(
        grads_kernel,
        out_shape=(part, part, jax.ShapeDtypeStruct((units,), F32)),
        in_specs=[spec(VMEM)] * 2,
        out_specs=(spec(VMEM),) * 3,
        compiler_params=pltpu.CompilerParams(vmem_limit_bytes=LIMIT),
    )(total, other)


def gather_small(block, send, add):
    after = lax.optimization_barrier
    swap = lambda value: send(value, lambda r, c: (r, c ^ 1))
    near_of = lambda r, c: lax.rem(c + 12 - 8 * r, 16)
    near = send(block, lambda r, c: (r, (c + (4 if r == 0 else 12)) % 16))
    far = send(row_half(block), lambda r, c: (r, c ^ 8))
    level = send(block, lambda r, c: (r, c ^ 2) if (c // 2) % 2 == r else None)
    beside = swap(block)
    acc = add([block, beside], [lambda r, c: c, lambda r, c: c ^ 1])
    near, acc = after((near, acc))
    cross = send(near, lambda r, c: (r, c ^ 2))
    level_beside = swap(level)
    near_beside = swap(near)
    over_x = send(far, lambda r, c: (1 - r, c))
    over_y = send(far, lambda r, c: (r, c ^ 2))
    over_d = send(far, lambda r, c: (1 - r, c ^ 2))
    cross_beside = swap(cross)
    acc = add([near, level], [near_of, lambda r, c: c ^ 2], acc)
    far_pair = bundle([(far, (0, ROW)), (over_x, (0, OTHER))], 1, (acc,))
    far_beside = swap(far_pair)
    acc = add([near_beside, level_beside, cross, far_pair], [lambda r, c: near_of(r, c) ^ 1, lambda r, c: c ^ 3, lambda r, c: near_of(r, c) ^ 2, lambda r, c: c ^ 8], acc)
    over_pair = bundle([(over_y, (0, ROW)), (over_d, (0, OTHER))], 1, (acc,))
    over_beside = swap(over_pair)
    acc = add([far_beside, cross_beside, over_pair], [lambda r, c: c ^ 9, lambda r, c: near_of(r, c) ^ 3, lambda r, c: c ^ 10], acc)
    acc = add([over_beside], [lambda r, c: c ^ 11], acc, True)
    return acc


def gather_ring(block, send, add, rows, cols, stops):
    held = send(block, lambda r, c: (r, (c + stops * r) % cols))
    held = jnp.where(lax.axis_index("row") == 0, block, held)
    acc = None
    for stop in range(stops):
        if stop:
            held = send(held, lambda r, c: (r, (c + 1) % cols))
        at = lambda r, c, stop=stop: lax.rem(c - stops * r - stop + 2 * cols, cols)
        acc = add([held], [at], acc)
    return acc


def on_device(
    features, self_weight, neigh_weight, bias, edge_tiles, tile_rows, tile_cols,
    tile_count, cotangent,
):
    rows = lax.axis_size("row")
    cols = lax.axis_size("col")
    stops = tile_count.shape[2]
    tiles = edge_tiles[0, 0]
    index = (tile_rows, tile_cols, tile_count)
    small = rows == 2 and cols == 16 and stops == 8

    def send(value, to):
        pairs = []
        for r in range(rows):
            for c in range(cols):
                goal = to(r, c)
                if goal is not None and goal != (r, c):
                    pairs.append((r * cols + c, goal[0] * cols + goal[1]))
        return lax.ppermute(value, ("row", "col"), pairs)

    def add(blocks, goals, acc=None, finish=False, cost=COST):
        return add_products(blocks, goals, index, stops, tiles, acc, finish, cost)

    if small:
        kept, away = gather_small(features, send, add)
        got = send(away, lambda r, c: (1 - r, c))
    else:
        acc = gather_ring(features, send, add, rows, cols, stops)
        kept = lax.psum_scatter(acc, "row", scatter_dimension=0, tiled=True)
        got = jnp.zeros_like(kept)
    output, keep, away = run_layer(
        features, kept, got, self_weight, neigh_weight, bias, cotangent
    )
    swap = lambda value: send(value, lambda r, c: (r, c ^ 1))
    total = keep + swap(away)
    if small:
        total = total + send(total, lambda r, c: (1 - r, c))
    else:
        total = lax.psum(total, "row")
    bit = 2
    while bit < cols:
        total = total + send(total, lambda r, c: (r, c ^ bit))
        bit *= 2
    return (output, *place_grads(total, swap(total)))


def solution(mesh):
    in_specs = (
        P("col", None, None),
        P(),
        P(),
        P(),
        P("row", "col", None, None, None),
        P("row", "col", None),
        P("row", "col", None),
        P("row", "col", None),
        P("col", "row", None),
    )
    out_specs = (P("col", "row", None), P(), P(), P())
    return jax.shard_map(
        on_device, mesh=mesh, in_specs=in_specs, out_specs=out_specs, check_vma=False
    )
```

```python
import functools

import jax
import jax.numpy as jnp
from jax import lax
from jax.experimental import pallas as pl
from jax.experimental.pallas import tpu as pltpu
from jax.sharding import PartitionSpec as P

VMEM = pltpu.VMEM
SMEM = pltpu.SMEM
F32 = jnp.float32
BF16 = jnp.bfloat16
LIMIT = 24 * 1024 * 1024
GROUP = 4
COST = 10


def split(value):
    high = value.astype(BF16)
    low = (value - high.astype(F32)).astype(BF16)
    return high, low


def dot3(left, right, dims):
    lh, ll = left
    rh, rl = right
    mul = functools.partial(
        lax.dot_general, dimension_numbers=(dims, ((), ())), preferred_element_type=F32
    )
    return mul(lh, rh) + (mul(lh, rl) + mul(ll, rh))


def spec(space):
    return pl.BlockSpec(memory_space=space)


def tiles_kernel(goals, pieces, has_acc, finish, slots, stops, rows, cols, counts, *refs):
    blocks = []
    for count in pieces:
        if count < 0:
            blocks += [(refs[0].at[at],) for at in range(-count)]
            refs = refs[1:]
        else:
            blocks.append(refs[:count])
            refs = refs[count:]
    tiles, refs = refs[0], refs[1:]
    if has_acc:
        acc_in, refs = refs[0], refs[1:]
    if finish:
        keep, send, acc, pair = refs
    else:
        acc, pair = refs
    row = lax.axis_index("row")
    col = lax.axis_index("col")
    across = lax.axis_size("col")
    if has_acc:
        acc[...] = acc_in[...]
    else:
        acc[...] = jnp.zeros_like(acc)
    width = acc.shape[1]
    side = tiles.shape[1]
    for goal, block in zip(goals, blocks):
        stop = lax.rem(col - stops * row - goal(row, col) + 2 * across, across)

        @pl.when(stop < stops)
        def _(block=block, stop=stop):
            for place, piece in enumerate(block):
                high, low = split(piece[...])
                size = high.shape[0]
                if len(block) == 1:
                    start = 0
                else:
                    start = pl.multiple_of((1 - row if place else row) * size, size)
                pair[pl.ds(start, size), :width] = high
                pair[pl.ds(start, size), width:] = low
            live = counts[0, 0, stop]
            base = stop * slots
            for first in range(0, slots, GROUP):
                here = range(first, min(first + GROUP, slots))

                @pl.when(first < live)
                def _(here=here):
                    prods = []
                    for t in here:
                        at = pl.multiple_of(cols[0, 0, base + t] * side, side)
                        both = jnp.dot(
                            tiles[base + t], pair[pl.ds(at, side), :],
                            preferred_element_type=F32,
                        )
                        prods.append(both[:, :width] + both[:, width:])
                    for t, prod in zip(here, prods):
                        at = pl.multiple_of(rows[0, 0, base + t] * side, side)
                        acc[pl.ds(at, side), :] += jnp.where(t < live, prod, 0.0)

    if finish:
        half = keep.shape[0]
        for out, place in ((keep, row), (send, 1 - row)):
            out[...] = acc[pl.ds(pl.multiple_of(place * half, half), half), :]


def add_products(blocks, goals, index, stops, tiles, acc, finish, cost):
    blocks = [b if isinstance(b, tuple) else (b,) for b in blocks]
    pieces = tuple(len(b) if len(b) > 1 else -b[0].shape[0] for b in blocks)
    flat = [piece for b in blocks for piece in b]
    n = len(goals)
    width = flat[0].shape[-1]
    nodes = max(len(b) * b[0].shape[-2] for b in blocks)
    slots = tiles.shape[0] // stops
    side = tiles.shape[1]
    whole = jax.ShapeDtypeStruct((nodes, width), F32)
    part = jax.ShapeDtypeStruct((nodes // 2, width), F32)
    body = functools.partial(
        tiles_kernel, tuple(goals), pieces, acc is not None, finish, slots, stops
    )
    scratch = [VMEM((nodes, 2 * width), BF16)]
    if finish:
        scratch = [VMEM((nodes, width), F32)] + scratch
    return pl.pallas_call(
        body,
        out_shape=(part, part) if finish else whole,
        in_specs=[spec(SMEM)] * 3
        + [spec(VMEM)] * (len(flat) + 1)
        + ([spec(VMEM)] if acc is not None else []),
        out_specs=(spec(VMEM),) * 2 if finish else spec(VMEM),
        scratch_shapes=scratch,
        compiler_params=pltpu.CompilerParams(vmem_limit_bytes=LIMIT),
        cost_estimate=pl.CostEstimate(
            flops=n * slots * side * side * width * cost,
            bytes_accessed=n * slots * side * side * 2,
            transcendentals=0,
        ),
    )(*index, *flat, tiles, *(() if acc is None else (acc,)))


def half_kernel(block, out):
    half = out.shape[0]
    row = lax.axis_index("row")
    at = pl.multiple_of(row * half, half)
    out[...] = block[0, pl.ds(at, half), :]


def row_half(block):
    _, nodes, width = block.shape
    return pl.pallas_call(
        half_kernel,
        out_shape=jax.ShapeDtypeStruct((nodes // 2, width), F32),
        in_specs=[spec(VMEM)],
        out_specs=spec(VMEM),
        compiler_params=pltpu.CompilerParams(vmem_limit_bytes=LIMIT),
    )(block)


ROW, OTHER = "row", "other"


def bundle_kernel(places, *refs):
    out = refs[-1]
    row = lax.axis_index("row")
    for ref, (block, half) in zip(refs, places):
        if half is None:
            out[block] = ref[0]
            continue
        size = ref.shape[0]
        half = {ROW: row, OTHER: 1 - row}.get(half, half)
        out[block, pl.ds(pl.multiple_of(half * size, size), size), :] = ref[...]


def bundle(pieces, blocks, after=()):
    piece, (_, half) = pieces[0]
    nodes, width = piece.shape[-2] * (1 if half is None else 2), piece.shape[-1]
    return pl.pallas_call(
        functools.partial(bundle_kernel, tuple(place for _, place in pieces)),
        out_shape=jax.ShapeDtypeStruct((blocks, nodes, width), F32),
        in_specs=[spec(VMEM)] * len(pieces) + [spec(pl.ANY)] * len(after),
        out_specs=spec(VMEM),
        compiler_params=pltpu.CompilerParams(vmem_limit_bytes=LIMIT),
        cost_estimate=pl.CostEstimate(
            flops=1024, bytes_accessed=8 * nodes * width * blocks, transcendentals=0
        ),
    )(*[piece for piece, _ in pieces], *after)


def layer_kernel(
    block, kept, got, self_weight, neigh_weight, bias, cotangent, output, keep, send
):
    depth = self_weight.shape[0]
    units = self_weight.shape[1]
    nodes = kept.shape[0]
    own = block[0, pl.ds(pl.multiple_of(lax.axis_index("row") * nodes, nodes), nodes), :]
    both = jnp.concatenate([own, kept[...] + got[...]], axis=1)
    inputs = split(both)
    weights = split(jnp.concatenate([self_weight[...], neigh_weight[...]], axis=0))
    pre = dot3(inputs, weights, ((1,), (0,))) + bias[...].reshape(1, units)
    root = 0.7978845608028654
    square = pre * pre
    bend = jnp.tanh(root * (pre + 0.044715 * (square * pre)))
    rise = 0.5 * (1.0 + bend)
    hidden = pre * rise
    scale = lax.rsqrt(jnp.mean(hidden * hidden, axis=-1, keepdims=True) + 1e-06)
    out = hidden * scale
    output[0] = out
    weight = cotangent[0]
    along = jnp.mean(weight * out, axis=-1, keepdims=True)
    slope = rise + (0.5 * root) * pre * (1.0 - bend * bend) * (
        1.0 + (3 * 0.044715) * square
    )
    back = scale * (weight - out * along) * slope
    grads = dot3(inputs, split(back), ((0,), (0,)))
    grad_bias = jnp.sum(back, axis=0, keepdims=True)
    first = lax.rem(lax.axis_index("col"), 2) == 0
    tail = jnp.broadcast_to(grad_bias, (8, units))
    keep[:depth, :] = jnp.where(first, grads[:depth], grads[depth:])
    send[:depth, :] = jnp.where(first, grads[depth:], grads[:depth])
    keep[depth:, :] = tail
    send[depth:, :] = tail


def run_layer(block, kept, got, self_weight, neigh_weight, bias, cotangent):
    nodes, depth = kept.shape
    units = self_weight.shape[1]
    part = jax.ShapeDtypeStruct((depth + 8, units), F32)
    return pl.pallas_call(
        layer_kernel,
        out_shape=(jax.ShapeDtypeStruct((1, nodes, units), F32), part, part),
        in_specs=[spec(VMEM)] * 7,
        out_specs=(spec(VMEM),) * 3,
        compiler_params=pltpu.CompilerParams(vmem_limit_bytes=LIMIT),
        cost_estimate=pl.CostEstimate(
            flops=12 * nodes * 2 * depth * units,
            bytes_accessed=nodes * units * 12,
            transcendentals=nodes * units,
        ),
    )(block, kept, got, self_weight, neigh_weight, bias, cotangent)


def grads_kernel(total, other, grad_self, grad_neigh, grad_bias):
    depth = grad_self.shape[0]
    first = lax.rem(lax.axis_index("col"), 2) == 0
    mine, theirs = total[:depth, :], other[:depth, :]
    grad_self[...] = jnp.where(first, mine, theirs)
    grad_neigh[...] = jnp.where(first, theirs, mine)
    grad_bias[...] = total[depth, :]


def place_grads(total, other):
    depth, units = total.shape[0] - 8, total.shape[1]
    part = jax.ShapeDtypeStruct((depth, units), F32)
    return pl.pallas_call(
        grads_kernel,
        out_shape=(part, part, jax.ShapeDtypeStruct((units,), F32)),
        in_specs=[spec(VMEM)] * 2,
        out_specs=(spec(VMEM),) * 3,
        compiler_params=pltpu.CompilerParams(vmem_limit_bytes=LIMIT),
    )(total, other)


def gather_small(block, send, add):
    after = lax.optimization_barrier
    swap = lambda value: send(value, lambda r, c: (r, c ^ 1))
    near_of = lambda r, c: lax.rem(c + 12 - 8 * r, 16)
    near = send(block, lambda r, c: (r, (c + (4 if r == 0 else 12)) % 16))
    far = send(row_half(block), lambda r, c: (r, c ^ 8))
    level = send(block, lambda r, c: (r, c ^ 2) if (c // 2) % 2 == r else None)
    beside = swap(block)
    acc = add([block, beside], [lambda r, c: c, lambda r, c: c ^ 1])
    near, acc = after((near, acc))
    cross = send(near, lambda r, c: (r, c ^ 2))
    level_beside = swap(level)
    near_beside = swap(near)
    over_x = send(far, lambda r, c: (1 - r, c))
    over_y = send(far, lambda r, c: (r, c ^ 2))
    over_d = send(far, lambda r, c: (1 - r, c ^ 2))
    cross_beside = swap(cross)
    acc = add([near, level], [near_of, lambda r, c: c ^ 2], acc)
    far_pair = bundle([(far, (0, ROW)), (over_x, (0, OTHER))], 1, (acc,))
    far_beside = swap(far_pair)
    acc = add([near_beside, level_beside, cross, far_pair], [lambda r, c: near_of(r, c) ^ 1, lambda r, c: c ^ 3, lambda r, c: near_of(r, c) ^ 2, lambda r, c: c ^ 8], acc)
    over_pair = bundle([(over_y, (0, ROW)), (over_d, (0, OTHER))], 1, (acc,))
    over_beside = swap(over_pair)
    acc = add([far_beside, cross_beside, over_pair], [lambda r, c: c ^ 9, lambda r, c: near_of(r, c) ^ 3, lambda r, c: c ^ 10], acc)
    acc = add([over_beside], [lambda r, c: c ^ 11], acc, True)
    return acc


def gather_ring(block, send, add, rows, cols, stops):
    held = send(block, lambda r, c: (r, (c + stops * r) % cols))
    held = jnp.where(lax.axis_index("row") == 0, block, held)
    acc = None
    for stop in range(stops):
        if stop:
            held = send(held, lambda r, c: (r, (c + 1) % cols))
        at = lambda r, c, stop=stop: lax.rem(c - stops * r - stop + 2 * cols, cols)
        acc = add([held], [at], acc)
    return acc


def on_device(
    features, self_weight, neigh_weight, bias, edge_tiles, tile_rows, tile_cols,
    tile_count, cotangent,
):
    rows = lax.axis_size("row")
    cols = lax.axis_size("col")
    stops = tile_count.shape[2]
    tiles = edge_tiles[0, 0]
    index = (tile_rows, tile_cols, tile_count)
    small = rows == 2 and cols == 16 and stops == 8

    def send(value, to):
        pairs = []
        for r in range(rows):
            for c in range(cols):
                goal = to(r, c)
                if goal is not None and goal != (r, c):
                    pairs.append((r * cols + c, goal[0] * cols + goal[1]))
        return lax.ppermute(value, ("row", "col"), pairs)

    def add(blocks, goals, acc=None, finish=False, cost=COST):
        return add_products(blocks, goals, index, stops, tiles, acc, finish, cost)

    if small:
        kept, away = gather_small(features, send, add)
        got = send(away, lambda r, c: (1 - r, c))
    else:
        acc = gather_ring(features, send, add, rows, cols, stops)
        kept = lax.psum_scatter(acc, "row", scatter_dimension=0, tiled=True)
        got = jnp.zeros_like(kept)
    output, keep, away = run_layer(
        features, kept, got, self_weight, neigh_weight, bias, cotangent
    )
    swap = lambda value: send(value, lambda r, c: (r, c ^ 1))
    total = keep + swap(away)
    if small:
        total = total + send(total, lambda r, c: (1 - r, c))
    else:
        total = lax.psum(total, "row")
    bit = 2
    while bit < cols:
        total = total + send(total, lambda r, c: (r, c ^ bit))
        bit *= 2
    return (output, *place_grads(total, swap(total)))


def solution(mesh):
    in_specs = (
        P("col", None, None),
        P(),
        P(),
        P(),
        P("row", "col", None, None, None),
        P("row", "col", None),
        P("row", "col", None),
        P("row", "col", None),
        P("col", "row", None),
    )
    out_specs = (P("col", "row", None), P(), P(), P())
    return jax.shard_map(
        on_device, mesh=mesh, in_specs=in_specs, out_specs=out_specs, check_vma=False
    )
```

```python
import functools

import jax
import jax.numpy as jnp
from jax import lax
from jax.experimental import pallas as pl
from jax.experimental.pallas import tpu as pltpu
from jax.sharding import PartitionSpec as P

VMEM = pltpu.VMEM
SMEM = pltpu.SMEM
F32 = jnp.float32
BF16 = jnp.bfloat16
LIMIT = 24 * 1024 * 1024
GROUP = 4
COST = 10


def split(value):
    high = value.astype(BF16)
    low = (value - high.astype(F32)).astype(BF16)
    return high, low


def dot3(left, right, dims):
    lh, ll = left
    rh, rl = right
    mul = functools.partial(
        lax.dot_general, dimension_numbers=(dims, ((), ())), preferred_element_type=F32
    )
    return mul(lh, rh) + (mul(lh, rl) + mul(ll, rh))


def spec(space):
    return pl.BlockSpec(memory_space=space)


def tiles_kernel(goals, pieces, has_acc, finish, slots, stops, rows, cols, counts, *refs):
    blocks = []
    for count in pieces:
        if count < 0:
            blocks += [(refs[0].at[at],) for at in range(-count)]
            refs = refs[1:]
        else:
            blocks.append(refs[:count])
            refs = refs[count:]
    tiles, refs = refs[0], refs[1:]
    if has_acc:
        acc_in, refs = refs[0], refs[1:]
    if finish:
        keep, send, acc, pair = refs
    else:
        acc, pair = refs
    row = lax.axis_index("row")
    col = lax.axis_index("col")
    across = lax.axis_size("col")
    if has_acc:
        acc[...] = acc_in[...]
    else:
        acc[...] = jnp.zeros_like(acc)
    width = acc.shape[1]
    side = tiles.shape[1]
    for goal, block in zip(goals, blocks):
        stop = lax.rem(col - stops * row - goal(row, col) + 2 * across, across)

        @pl.when(stop < stops)
        def _(block=block, stop=stop):
            for place, piece in enumerate(block):
                high, low = split(piece[...])
                size = high.shape[0]
                if len(block) == 1:
                    start = 0
                else:
                    start = pl.multiple_of((1 - row if place else row) * size, size)
                pair[pl.ds(start, size), :width] = high
                pair[pl.ds(start, size), width:] = low
            live = counts[0, 0, stop]
            base = stop * slots
            for first in range(0, slots, GROUP):
                here = range(first, min(first + GROUP, slots))

                @pl.when(first < live)
                def _(here=here):
                    prods = []
                    for t in here:
                        at = pl.multiple_of(cols[0, 0, base + t] * side, side)
                        both = jnp.dot(
                            tiles[base + t], pair[pl.ds(at, side), :],
                            preferred_element_type=F32,
                        )
                        prods.append(both[:, :width] + both[:, width:])
                    for t, prod in zip(here, prods):
                        at = pl.multiple_of(rows[0, 0, base + t] * side, side)
                        acc[pl.ds(at, side), :] += jnp.where(t < live, prod, 0.0)

    if finish:
        half = keep.shape[0]
        for out, place in ((keep, row), (send, 1 - row)):
            out[...] = acc[pl.ds(pl.multiple_of(place * half, half), half), :]


def add_products(blocks, goals, index, stops, tiles, acc, finish, cost):
    blocks = [b if isinstance(b, tuple) else (b,) for b in blocks]
    pieces = tuple(len(b) if len(b) > 1 else -b[0].shape[0] for b in blocks)
    flat = [piece for b in blocks for piece in b]
    n = len(goals)
    width = flat[0].shape[-1]
    nodes = max(len(b) * b[0].shape[-2] for b in blocks)
    slots = tiles.shape[0] // stops
    side = tiles.shape[1]
    whole = jax.ShapeDtypeStruct((nodes, width), F32)
    part = jax.ShapeDtypeStruct((nodes // 2, width), F32)
    body = functools.partial(
        tiles_kernel, tuple(goals), pieces, acc is not None, finish, slots, stops
    )
    scratch = [VMEM((nodes, 2 * width), BF16)]
    if finish:
        scratch = [VMEM((nodes, width), F32)] + scratch
    return pl.pallas_call(
        body,
        out_shape=(part, part) if finish else whole,
        in_specs=[spec(SMEM)] * 3
        + [spec(VMEM)] * (len(flat) + 1)
        + ([spec(VMEM)] if acc is not None else []),
        out_specs=(spec(VMEM),) * 2 if finish else spec(VMEM),
        scratch_shapes=scratch,
        compiler_params=pltpu.CompilerParams(vmem_limit_bytes=LIMIT),
        cost_estimate=pl.CostEstimate(
            flops=n * slots * side * side * width * cost,
            bytes_accessed=n * slots * side * side * 2,
            transcendentals=0,
        ),
    )(*index, *flat, tiles, *(() if acc is None else (acc,)))


def half_kernel(block, out):
    half = out.shape[0]
    row = lax.axis_index("row")
    at = pl.multiple_of(row * half, half)
    out[...] = block[0, pl.ds(at, half), :]


def row_half(block):
    _, nodes, width = block.shape
    return pl.pallas_call(
        half_kernel,
        out_shape=jax.ShapeDtypeStruct((nodes // 2, width), F32),
        in_specs=[spec(VMEM)],
        out_specs=spec(VMEM),
        compiler_params=pltpu.CompilerParams(vmem_limit_bytes=LIMIT),
    )(block)


ROW, OTHER = "row", "other"


def bundle_kernel(places, *refs):
    out = refs[-1]
    row = lax.axis_index("row")
    for ref, (block, half) in zip(refs, places):
        if half is None:
            out[block] = ref[0]
            continue
        size = ref.shape[0]
        half = {ROW: row, OTHER: 1 - row}.get(half, half)
        out[block, pl.ds(pl.multiple_of(half * size, size), size), :] = ref[...]


def bundle(pieces, blocks, after=()):
    piece, (_, half) = pieces[0]
    nodes, width = piece.shape[-2] * (1 if half is None else 2), piece.shape[-1]
    return pl.pallas_call(
        functools.partial(bundle_kernel, tuple(place for _, place in pieces)),
        out_shape=jax.ShapeDtypeStruct((blocks, nodes, width), F32),
        in_specs=[spec(VMEM)] * len(pieces) + [spec(pl.ANY)] * len(after),
        out_specs=spec(VMEM),
        compiler_params=pltpu.CompilerParams(vmem_limit_bytes=LIMIT),
        cost_estimate=pl.CostEstimate(
            flops=1024, bytes_accessed=8 * nodes * width * blocks, transcendentals=0
        ),
    )(*[piece for piece, _ in pieces], *after)


def own_kernel(block, self_weight, bias, out):
    nodes, units = out.shape
    own = block[0, pl.ds(pl.multiple_of(lax.axis_index("row") * nodes, nodes), nodes), :]
    out[...] = dot3(split(own), split(self_weight[...]), ((1,), (0,))) + bias[
        ...
    ].reshape(1, units)


def layer_kernel(
    block, kept, got, from_own, neigh_weight, cotangent, output, keep, send
):
    depth = neigh_weight.shape[0]
    units = neigh_weight.shape[1]
    nodes = kept.shape[0]
    own = block[0, pl.ds(pl.multiple_of(lax.axis_index("row") * nodes, nodes), nodes), :]
    aggregate = split(kept[...] + got[...])
    inputs = [
        jnp.concatenate(parts, axis=1) for parts in zip(split(own), aggregate)
    ]
    pre = from_own[...] + dot3(aggregate, split(neigh_weight[...]), ((1,), (0,)))
    root = 0.7978845608028654
    square = pre * pre
    bend = jnp.tanh(root * (pre + 0.044715 * (square * pre)))
    rise = 0.5 * (1.0 + bend)
    hidden = pre * rise
    scale = lax.rsqrt(jnp.mean(hidden * hidden, axis=-1, keepdims=True) + 1e-06)
    out = hidden * scale
    output[0] = out
    weight = cotangent[0]
    along = jnp.mean(weight * out, axis=-1, keepdims=True)
    slope = rise + (0.5 * root) * pre * (1.0 - bend * bend) * (
        1.0 + (3 * 0.044715) * square
    )
    back = scale * (weight - out * along) * slope
    grads = dot3(inputs, split(back), ((0,), (0,)))
    grad_bias = jnp.sum(back, axis=0, keepdims=True)
    first = lax.rem(lax.axis_index("col"), 2) == 0
    tail = jnp.broadcast_to(grad_bias, (8, units))
    keep[:depth, :] = jnp.where(first, grads[:depth], grads[depth:])
    send[:depth, :] = jnp.where(first, grads[depth:], grads[:depth])
    keep[depth:, :] = tail
    send[depth:, :] = tail


def run_layer(block, kept, got, self_weight, neigh_weight, bias, cotangent):
    nodes, depth = kept.shape
    units = self_weight.shape[1]
    part = jax.ShapeDtypeStruct((depth + 8, units), F32)
    from_own = pl.pallas_call(
        own_kernel,
        out_shape=jax.ShapeDtypeStruct((nodes, units), F32),
        in_specs=[spec(VMEM)] * 3,
        out_specs=spec(VMEM),
        compiler_params=pltpu.CompilerParams(vmem_limit_bytes=LIMIT),
        cost_estimate=pl.CostEstimate(
            flops=6 * nodes * depth * units,
            bytes_accessed=nodes * units * 4,
            transcendentals=0,
        ),
    )(block, self_weight, bias)
    return pl.pallas_call(
        layer_kernel,
        out_shape=(jax.ShapeDtypeStruct((1, nodes, units), F32), part, part),
        in_specs=[spec(VMEM)] * 6,
        out_specs=(spec(VMEM),) * 3,
        compiler_params=pltpu.CompilerParams(vmem_limit_bytes=LIMIT),
        cost_estimate=pl.CostEstimate(
            flops=12 * nodes * 2 * depth * units,
            bytes_accessed=nodes * units * 12,
            transcendentals=nodes * units,
        ),
    )(block, kept, got, from_own, neigh_weight, cotangent)


def grads_kernel(total, other, grad_self, grad_neigh, grad_bias):
    depth = grad_self.shape[0]
    first = lax.rem(lax.axis_index("col"), 2) == 0
    mine, theirs = total[:depth, :], other[:depth, :]
    grad_self[...] = jnp.where(first, mine, theirs)
    grad_neigh[...] = jnp.where(first, theirs, mine)
    grad_bias[...] = total[depth, :]


def place_grads(total, other):
    depth, units = total.shape[0] - 8, total.shape[1]
    part = jax.ShapeDtypeStruct((depth, units), F32)
    return pl.pallas_call(
        grads_kernel,
        out_shape=(part, part, jax.ShapeDtypeStruct((units,), F32)),
        in_specs=[spec(VMEM)] * 2,
        out_specs=(spec(VMEM),) * 3,
        compiler_params=pltpu.CompilerParams(vmem_limit_bytes=LIMIT),
    )(total, other)


def gather_small(block, send, add):
    after = lax.optimization_barrier
    swap = lambda value: send(value, lambda r, c: (r, c ^ 1))
    near_of = lambda r, c: lax.rem(c + 12 - 8 * r, 16)
    near = send(block, lambda r, c: (r, (c + (4 if r == 0 else 12)) % 16))
    far = send(row_half(block), lambda r, c: (r, c ^ 8))
    level = send(block, lambda r, c: (r, c ^ 2) if (c // 2) % 2 == r else None)
    beside = swap(block)
    acc = add([block, beside], [lambda r, c: c, lambda r, c: c ^ 1])
    near, acc = after((near, acc))
    cross = send(near, lambda r, c: (r, c ^ 2))
    level_beside = swap(level)
    near_beside = swap(near)
    over_x = send(far, lambda r, c: (1 - r, c))
    over_y = send(far, lambda r, c: (r, c ^ 2))
    over_d = send(far, lambda r, c: (1 - r, c ^ 2))
    cross_beside = swap(cross)
    acc = add([near, level], [near_of, lambda r, c: c ^ 2], acc)
    far_pair = bundle([(far, (0, ROW)), (over_x, (0, OTHER))], 1, (acc,))
    far_beside = swap(far_pair)
    acc = add([near_beside, level_beside, cross, far_pair], [lambda r, c: near_of(r, c) ^ 1, lambda r, c: c ^ 3, lambda r, c: near_of(r, c) ^ 2, lambda r, c: c ^ 8], acc)
    over_pair = bundle([(over_y, (0, ROW)), (over_d, (0, OTHER))], 1, (acc,))
    over_beside = swap(over_pair)
    acc = add([far_beside, cross_beside, over_pair], [lambda r, c: c ^ 9, lambda r, c: near_of(r, c) ^ 3, lambda r, c: c ^ 10], acc)
    acc = add([over_beside], [lambda r, c: c ^ 11], acc, True)
    return acc


def gather_ring(block, send, add, rows, cols, stops):
    held = send(block, lambda r, c: (r, (c + stops * r) % cols))
    held = jnp.where(lax.axis_index("row") == 0, block, held)
    acc = None
    for stop in range(stops):
        if stop:
            held = send(held, lambda r, c: (r, (c + 1) % cols))
        at = lambda r, c, stop=stop: lax.rem(c - stops * r - stop + 2 * cols, cols)
        acc = add([held], [at], acc)
    return acc


def on_device(
    features, self_weight, neigh_weight, bias, edge_tiles, tile_rows, tile_cols,
    tile_count, cotangent,
):
    rows = lax.axis_size("row")
    cols = lax.axis_size("col")
    stops = tile_count.shape[2]
    tiles = edge_tiles[0, 0]
    index = (tile_rows, tile_cols, tile_count)
    small = rows == 2 and cols == 16 and stops == 8

    def send(value, to):
        pairs = []
        for r in range(rows):
            for c in range(cols):
                goal = to(r, c)
                if goal is not None and goal != (r, c):
                    pairs.append((r * cols + c, goal[0] * cols + goal[1]))
        return lax.ppermute(value, ("row", "col"), pairs)

    def add(blocks, goals, acc=None, finish=False, cost=COST):
        return add_products(blocks, goals, index, stops, tiles, acc, finish, cost)

    if small:
        kept, away = gather_small(features, send, add)
        got = send(away, lambda r, c: (1 - r, c))
    else:
        acc = gather_ring(features, send, add, rows, cols, stops)
        kept = lax.psum_scatter(acc, "row", scatter_dimension=0, tiled=True)
        got = jnp.zeros_like(kept)
    output, keep, away = run_layer(
        features, kept, got, self_weight, neigh_weight, bias, cotangent
    )
    swap = lambda value: send(value, lambda r, c: (r, c ^ 1))
    total = keep + swap(away)
    if small:
        total = total + send(total, lambda r, c: (1 - r, c))
    else:
        total = lax.psum(total, "row")
    bit = 2
    while bit < cols:
        total = total + send(total, lambda r, c: (r, c ^ bit))
        bit *= 2
    return (output, *place_grads(total, swap(total)))


def solution(mesh):
    in_specs = (
        P("col", None, None),
        P(),
        P(),
        P(),
        P("row", "col", None, None, None),
        P("row", "col", None),
        P("row", "col", None),
        P("row", "col", None),
        P("col", "row", None),
    )
    out_specs = (P("col", "row", None), P(), P(), P())
    return jax.shard_map(
        on_device, mesh=mesh, in_specs=in_specs, out_specs=out_specs, check_vma=False
    )
```
